32 devices in a mesh: prow: 8 (over z, core), pcol: 4 (over y, x).
Axes of the slice: x: 2, y: 2, z: 4, core: 2. Of those that a mesh axis runs over, the one named last changes fastest.
Arguments:
- kernel: float32 [6, 8, 256, 12, 4, 256], P(None, 'prow', None, None, 'pcol'), as said below
Outputs:
- factored: float32 [6, 8, 256, 12, 4, 256], P(None, 'prow', None, None, 'pcol')
Inputs may be any that keep to these rules, and one draw needn't show every extreme that they name: kernel is symmetric (entry (a, b) equals entry (b, a)); every diagonal entry is 1.1, every off-diagonal entry lies in (0, 1], and the matrix is positive definite with smallest eigenvalue at least 0.1.
All inputs are finite; a program needn't handle non-finite values.
Results may differ from the reference program's by a relative error of at most 0.0003.
Values sent between devices are 32-bit elements; how exact they have to be, the bound alone decides.
A program may use at most 128 MiB of HBM per device.

```python
import jax
import jax.numpy as jnp
from jax import lax

NMAT = 12288
BLK = 256
STEPS = 2
LBR = 6
LBC = 12


def draw_kernel(key, part):
    feature_count = 8
    positions = jax.random.normal(key, (NMAT, feature_count), jnp.float32)
    squared = jnp.zeros((NMAT, NMAT), jnp.float32)
    for column in range(feature_count):
        coordinate = positions[:, column]
        difference = coordinate[:, None] - coordinate[None, :]
        squared = squared + difference * difference
    kernel_vals = jnp.exp(squared * (-1.0 / feature_count))
    counter = jnp.arange(NMAT, dtype=jnp.int32)
    on_diag = counter[:, None] == counter[None, :]
    full = kernel_vals + jnp.where(on_diag, 0.1, 0.0).astype(jnp.float32)
    return full.reshape(LBR, NMAT // (LBR * BLK), BLK, LBC, NMAT // (LBC * BLK), BLK)


def setup_inputs(seed: int = 0) -> dict:
    keys = jax.random.split(jax.random.key(seed), 2)
    kernel = draw_kernel(jax.random.fold_in(keys[1], 71), 0)
    return {"kernel": kernel}


def reference(kernel):
    full = kernel.reshape(NMAT, NMAT)
    eye = jnp.eye(BLK, dtype=full.dtype)
    for k in range(STEPS):
        low = k * BLK
        high = low + BLK
        lower = jnp.linalg.cholesky(full[low:high, low:high])
        inverse = jax.scipy.linalg.solve_triangular(lower, eye, lower=True)
        product = jnp.dot(full[high:, low:high], inverse.T, precision=lax.Precision.HIGHEST)
        trailing = full[high:, high:] - jnp.dot(product, product.T, precision=lax.Precision.HIGHEST)
        full = full.at[low:high, low:high].set(lower)
        full = full.at[high:, low:high].set(product)
        full = full.at[low:high, high:].set(0.0)
        full = full.at[high:, high:].set(trailing)
    return full.reshape(kernel.shape)
```

```python
import functools

import jax
import jax.numpy as jnp
from jax import lax
from jax.experimental import pallas as pl
from jax.experimental.pallas import tpu as pltpu
from jax.sharding import PartitionSpec as P

STEPS = 2
TILE = 128
SUB = 8
HIGH = lax.Precision.HIGHEST


def dot_nn(a, b):
    return lax.dot_general(
        a, b, (((1,), (0,)), ((), ())), precision=HIGH, preferred_element_type=jnp.float32
    )


def dot_nt(a, b):
    return lax.dot_general(
        a, b, (((1,), (1,)), ((), ())), precision=HIGH, preferred_element_type=jnp.float32
    )


def split(x):
    hi = x.astype(jnp.bfloat16)
    lo = (x - hi.astype(jnp.float32)).astype(jnp.bfloat16)
    return hi, lo


def factor_tile(tile):
    count = TILE // SUB
    row = lax.broadcasted_iota(jnp.int32, (SUB, TILE), 0)
    lane = lax.broadcasted_iota(jnp.int32, (SUB, TILE), 1)
    upper = [tile[SUB * r : SUB * (r + 1), :] for r in range(count)]
    inverse = [jnp.where(lane == row + SUB * r, 1.0, 0.0) for r in range(count)]
    for g in range(count):
        cols = [
            [
                jnp.broadcast_to(upper[r][:, SUB * g + j : SUB * g + j + 1], (SUB, TILE))
                for r in range(g, count)
            ]
            for j in range(SUB)
        ]
        scale = jnp.zeros((SUB, TILE), jnp.float32)
        for j in range(SUB):
            pivot = jnp.broadcast_to(cols[j][0][j : j + 1, :], (SUB, TILE))
            scale = jnp.where(row == j, pivot, scale)
            recip = 1.0 / pivot
            row_u = jnp.broadcast_to(upper[g][j : j + 1, :], (SUB, TILE)) * recip
            row_i = jnp.broadcast_to(inverse[g][j : j + 1, :], (SUB, TILE)) * recip
            heads = [
                jnp.broadcast_to(cols[j2][0][j : j + 1, :], (SUB, TILE)) * recip
                for j2 in range(j + 1, SUB)
            ]
            for r in range(g, count):
                f = cols[j][r - g]
                if r == g:
                    f = jnp.where(row > j, f, 0.0)
                upper[r] = upper[r] - f * row_u
                inverse[r] = inverse[r] - f * row_i
                for j2 in range(j + 1, SUB):
                    cols[j2][r - g] = cols[j2][r - g] - f * heads[j2 - j - 1]
        root = lax.rsqrt(scale)
        upper[g] = jnp.where(lane >= row + SUB * g, upper[g] * root, 0.0)
        inverse[g] = jnp.where(lane <= row + SUB * g, inverse[g] * root, 0.0)
    return jnp.concatenate(upper, axis=0), jnp.concatenate(inverse, axis=0)


def factor_kernel(d_ref, l_ref, w_ref, work):
    n = d_ref.shape[0]
    work[...] = d_ref[...]
    l_ref[...] = jnp.zeros_like(l_ref)
    w_ref[...] = jnp.where(
        lax.broadcasted_iota(jnp.int32, (n, n), 0) == lax.broadcasted_iota(jnp.int32, (n, n), 1),
        1.0,
        0.0,
    )
    rows = lax.broadcasted_iota(jnp.int32, (n, TILE), 0)

    def step(t, carry):
        at = pl.ds(pl.multiple_of(t * TILE, TILE), TILE)
        upper, inverse = factor_tile(work[at, at])
        panel = dot_nt(work[:, at], inverse)
        below = jnp.where(rows >= (t + 1) * TILE, panel, 0.0)
        l_ref[:, at] = below
        l_ref[at, at] = upper.T
        work[...] = work[...] - dot_nt(below, below)
        head = dot_nn(inverse, w_ref[at, :])
        w_ref[...] = w_ref[...] - dot_nn(below, head)
        w_ref[at, :] = head
        return carry

    lax.fori_loop(0, n // TILE, step, 0)


def factor(diag):
    n = diag.shape[0]
    out = jax.ShapeDtypeStruct((n, n), jnp.float32)
    return pl.pallas_call(
        factor_kernel,
        out_shape=(out, out),
        in_specs=[pl.BlockSpec(memory_space=pltpu.VMEM)],
        out_specs=(pl.BlockSpec(memory_space=pltpu.VMEM),) * 2,
        scratch_shapes=[pltpu.VMEM((n, n), jnp.float32)],
        compiler_params=pltpu.CompilerParams(vmem_limit_bytes=32 * 2**20),
        cost_estimate=pl.CostEstimate(flops=2 * n**3, bytes_accessed=12 * n * n, transcendentals=0),
    )(diag)


def update_kernel(rows, blk, lbc, m_ref, r_ref, c_ref, w_ref, l_ref, out_ref, cols):
    a = pl.program_id(0)
    row_id = a * rows + lax.axis_index("prow")
    q = lax.axis_index("pcol")
    lanes = blk // TILE
    pitch = lbc * lanes
    depth = STEPS * blk

    @pl.when(a == 0)
    def _():
        def prepare(b, carry):
            raw = jnp.concatenate([c_ref[k, b] for k in range(STEPS)], axis=0)
            hi, lo = split(dot_nn(w_ref[...], raw))
            cols[b, 0:depth, :] = hi
            cols[b, depth : 2 * depth, :] = hi
            cols[b, 2 * depth : 3 * depth, :] = lo
            return carry

        lax.fori_loop(0, lbc, prepare, 0)

    def store(b, value):
        for h in range(lanes):
            at = pl.ds(lanes * b + h, blk, stride=pitch)
            out_ref[at, :] = value[:, h * TILE : (h + 1) * TILE]

    @pl.when(row_id < STEPS)
    def _():
        out_ref[...] = jnp.zeros_like(out_ref)
        for i in range(STEPS):
            for j in range(i + 1):

                @pl.when((row_id == i) & (q == j))
                def _():
                    store(0, l_ref[i * blk : (i + 1) * blk, j * blk : (j + 1) * blk])

    @pl.when(row_id >= STEPS)
    def _():
        raw = jnp.concatenate([r_ref[k, 0] for k in range(STEPS)], axis=1)
        panel = dot_nt(raw, w_ref[...])
        hi, lo = split(panel)
        left = jnp.concatenate([hi, lo, hi], axis=1)
        for b in range(lbc):
            delta = jnp.dot(left, cols[b], preferred_element_type=jnp.float32)
            for h in range(lanes):
                at = pl.ds(lanes * b + h, blk, stride=pitch)
                out_ref[at, :] = m_ref[at, :] - delta[:, h * TILE : (h + 1) * TILE]
        for j in range(STEPS):

            @pl.when(q == j)
            def _():
                store(0, panel[:, j * blk : (j + 1) * blk])


def update(flat, row_panel, col_panel, inverse, lower, rows):
    _, lbr, blk, _ = row_panel.shape
    lbc = col_panel.shape[1]
    depth = STEPS * blk
    stripe = blk * lbc * (blk // TILE)
    whole = pl.BlockSpec((depth, depth), lambda a: (0, 0))
    return pl.pallas_call(
        functools.partial(update_kernel, rows, blk, lbc),
        grid=(lbr,),
        out_shape=jax.ShapeDtypeStruct(flat.shape, jnp.float32),
        in_specs=[
            pl.BlockSpec((stripe, TILE), lambda a: (a, 0)),
            pl.BlockSpec((STEPS, 1, blk, blk), lambda a: (0, a, 0, 0)),
            pl.BlockSpec((STEPS, lbc, blk, blk), lambda a: (0, 0, 0, 0)),
            whole,
            whole,
        ],
        out_specs=pl.BlockSpec((stripe, TILE), lambda a: (a, 0)),
        scratch_shapes=[pltpu.VMEM((lbc, 3 * depth, blk), jnp.bfloat16)],
        compiler_params=pltpu.CompilerParams(vmem_limit_bytes=56 * 2**20),
        cost_estimate=pl.CostEstimate(
            flops=6 * flat.size * depth, bytes_accessed=8 * flat.size, transcendentals=0
        ),
    )(flat, row_panel, col_panel, inverse, lower)


def on_device(kernel):
    rows = lax.axis_size("prow")
    p = lax.axis_index("prow")
    q = lax.axis_index("pcol")
    lbr, blk, lbc = (kernel.shape[0], kernel.shape[2], kernel.shape[3])
    flat = kernel.reshape(lbr * blk * lbc * (blk // TILE), TILE)
    column = kernel[:, 0, :, 0, 0, :]
    across = kernel[0, 0, :, :, 0, :].transpose(1, 0, 2)

    blocks = [
        jnp.where((p == i) & (q == j), column[0], 0.0) for i in range(STEPS) for j in range(i + 1)
    ]
    d00, d10, d11 = lax.psum(jnp.stack(blocks), ("prow", "pcol"))
    diag = jnp.block([[d00, d10.T], [d10, d11]])
    row_panel = lax.psum(
        jnp.stack([jnp.where(q == k, column, 0.0) for k in range(STEPS)]), "pcol"
    )
    col_panel = lax.psum(
        jnp.stack([jnp.where(p == k, across, 0.0) for k in range(STEPS)]), "prow"
    )
    lower, inverse = factor(diag)
    out = update(flat, row_panel, col_panel, inverse, lower, rows)
    return out.reshape(kernel.shape)


def solution(mesh):
    in_specs = (P(None, "prow", None, None, "pcol", None),)
    out_specs = P(None, "prow", None, None, "pcol", None)
    return jax.shard_map(
        on_device, mesh=mesh, in_specs=in_specs, out_specs=out_specs, check_vma=False
    )
```

```python
import functools

import jax
import jax.numpy as jnp
from jax import lax
from jax.experimental import pallas as pl
from jax.experimental.pallas import tpu as pltpu
from jax.sharding import PartitionSpec as P

STEPS = 2
TILE = 128
SUB = 8
HIGH = lax.Precision.HIGHEST


def dot_nn(a, b):
    return lax.dot_general(
        a, b, (((1,), (0,)), ((), ())), precision=HIGH, preferred_element_type=jnp.float32
    )


def dot_nt(a, b):
    return lax.dot_general(
        a, b, (((1,), (1,)), ((), ())), precision=HIGH, preferred_element_type=jnp.float32
    )


def split(x):
    hi = x.astype(jnp.bfloat16)
    lo = (x - hi.astype(jnp.float32)).astype(jnp.bfloat16)
    return hi, lo


def factor_tile(tile):
    count = TILE // SUB
    row = lax.broadcasted_iota(jnp.int32, (SUB, TILE), 0)
    lane = lax.broadcasted_iota(jnp.int32, (SUB, TILE), 1)
    upper = [tile[SUB * r : SUB * (r + 1), :] for r in range(count)]
    inverse = [jnp.where(lane == row + SUB * r, 1.0, 0.0) for r in range(count)]
    for g in range(count):
        cols = [
            [
                jnp.broadcast_to(upper[r][:, SUB * g + j : SUB * g + j + 1], (SUB, TILE))
                for r in range(g, count)
            ]
            for j in range(SUB)
        ]
        scale = jnp.zeros((SUB, TILE), jnp.float32)
        for j in range(SUB):
            pivot = jnp.broadcast_to(cols[j][0][j : j + 1, :], (SUB, TILE))
            scale = jnp.where(row == j, pivot, scale)
            recip = 1.0 / pivot
            row_u = jnp.broadcast_to(upper[g][j : j + 1, :], (SUB, TILE)) * recip
            row_i = jnp.broadcast_to(inverse[g][j : j + 1, :], (SUB, TILE)) * recip
            heads = [
                jnp.broadcast_to(cols[j2][0][j : j + 1, :], (SUB, TILE)) * recip
                for j2 in range(j + 1, SUB)
            ]
            for r in range(g, count):
                f = cols[j][r - g]
                if r == g:
                    f = jnp.where(row > j, f, 0.0)
                upper[r] = upper[r] - f * row_u
                inverse[r] = inverse[r] - f * row_i
                for j2 in range(j + 1, SUB):
                    cols[j2][r - g] = cols[j2][r - g] - f * heads[j2 - j - 1]
        root = lax.rsqrt(scale)
        upper[g] = jnp.where(lane >= row + SUB * g, upper[g] * root, 0.0)
        inverse[g] = jnp.where(lane <= row + SUB * g, inverse[g] * root, 0.0)
    return jnp.concatenate(upper, axis=0), jnp.concatenate(inverse, axis=0)


def factor_kernel(d_ref, l_ref, w_ref, work):
    n = d_ref.shape[0]
    work[...] = d_ref[...]
    l_ref[...] = jnp.zeros_like(l_ref)
    w_ref[...] = jnp.where(
        lax.broadcasted_iota(jnp.int32, (n, n), 0) == lax.broadcasted_iota(jnp.int32, (n, n), 1),
        1.0,
        0.0,
    )
    rows = lax.broadcasted_iota(jnp.int32, (n, TILE), 0)

    def step(t, carry):
        at = pl.ds(pl.multiple_of(t * TILE, TILE), TILE)
        upper, inverse = factor_tile(work[at, at])
        panel = dot_nt(work[:, at], inverse)
        below = jnp.where(rows >= (t + 1) * TILE, panel, 0.0)
        l_ref[:, at] = below
        l_ref[at, at] = upper.T
        work[...] = work[...] - dot_nt(below, below)
        head = dot_nn(inverse, w_ref[at, :])
        w_ref[...] = w_ref[...] - dot_nn(below, head)
        w_ref[at, :] = head
        return carry

    lax.fori_loop(0, n // TILE, step, 0)


def factor(diag):
    n = diag.shape[0]
    out = jax.ShapeDtypeStruct((n, n), jnp.float32)
    return pl.pallas_call(
        factor_kernel,
        out_shape=(out, out),
        in_specs=[pl.BlockSpec(memory_space=pltpu.VMEM)],
        out_specs=(pl.BlockSpec(memory_space=pltpu.VMEM),) * 2,
        scratch_shapes=[pltpu.VMEM((n, n), jnp.float32)],
        compiler_params=pltpu.CompilerParams(vmem_limit_bytes=32 * 2**20),
        cost_estimate=pl.CostEstimate(flops=2 * n**3, bytes_accessed=12 * n * n, transcendentals=0),
    )(diag)


def update_kernel(rows, blk, lbc, m_ref, r_ref, c_ref, w_ref, l_ref, out_ref, cols):
    a = pl.program_id(0)
    row_id = a * rows + lax.axis_index("prow")
    q = lax.axis_index("pcol")
    lanes = blk // TILE
    pitch = lbc * lanes
    depth = STEPS * blk

    @pl.when(a == 0)
    def _():
        def prepare(b, carry):
            raw = jnp.concatenate([c_ref[k, b] for k in range(STEPS)], axis=0)
            hi, lo = split(dot_nn(w_ref[...], raw))
            cols[b, 0:depth, :] = hi
            cols[b, depth : 2 * depth, :] = hi
            cols[b, 2 * depth : 3 * depth, :] = lo
            return carry

        lax.fori_loop(0, lbc, prepare, 0)

    def store(b, value):
        for h in range(lanes):
            at = pl.ds(lanes * b + h, blk, stride=pitch)
            out_ref[at, :] = value[:, h * TILE : (h + 1) * TILE]

    @pl.when(row_id < STEPS)
    def _():
        out_ref[...] = jnp.zeros_like(out_ref)
        for i in range(STEPS):
            for j in range(i + 1):

                @pl.when((row_id == i) & (q == j))
                def _():
                    store(0, l_ref[i * blk : (i + 1) * blk, j * blk : (j + 1) * blk])

    @pl.when(row_id >= STEPS)
    def _():
        raw = jnp.concatenate([r_ref[k, 0] for k in range(STEPS)], axis=1)
        panel = dot_nt(raw, w_ref[...])
        hi, lo = split(panel)
        left = jnp.concatenate([hi, lo, hi], axis=1)
        for b in range(lbc):
            delta = jnp.dot(left, cols[b], preferred_element_type=jnp.float32)
            for h in range(lanes):
                at = pl.ds(lanes * b + h, blk, stride=pitch)
                out_ref[at, :] = m_ref[at, :] - delta[:, h * TILE : (h + 1) * TILE]
        for j in range(STEPS):

            @pl.when(q == j)
            def _():
                store(0, panel[:, j * blk : (j + 1) * blk])


def update(flat, row_panel, col_panel, inverse, lower, rows):
    blk = row_panel.shape[2]
    lbc = col_panel.shape[1]
    depth = STEPS * blk
    stripe = blk * lbc * (blk // TILE)
    lbr = flat.shape[0] // stripe
    whole = pl.BlockSpec((depth, depth), lambda a: (0, 0))
    return pl.pallas_call(
        functools.partial(update_kernel, rows, blk, lbc),
        grid=(lbr,),
        out_shape=jax.ShapeDtypeStruct(flat.shape, jnp.float32),
        in_specs=[
            pl.BlockSpec((stripe, TILE), lambda a: (a, 0)),
            pl.BlockSpec((STEPS, 1, blk, blk), lambda a: (0, a, 0, 0)),
            pl.BlockSpec((STEPS, lbc, blk, blk), lambda a: (0, 0, 0, 0)),
            whole,
            whole,
        ],
        out_specs=pl.BlockSpec((stripe, TILE), lambda a: (a, 0)),
        scratch_shapes=[pltpu.VMEM((lbc, 3 * depth, blk), jnp.bfloat16)],
        compiler_params=pltpu.CompilerParams(vmem_limit_bytes=56 * 2**20),
        cost_estimate=pl.CostEstimate(
            flops=6 * flat.size * depth, bytes_accessed=8 * flat.size, transcendentals=0
        ),
    )(flat, row_panel, col_panel, inverse, lower)


def copy_kernel(rows, cols, column, across, r_out, c_out, r_recv, c_recv, r_send, z_send, pair_send):
    lbr, lbc = column.shape[0], across.shape[0]
    bits = cols.bit_length() - 1
    p = lax.axis_index("prow")
    q = lax.axis_index("pcol")
    own = p % 2
    other = 1 - own
    pair = p + 1 - 2 * own
    has_next = p + 2 < rows

    def flipped(value, bit):
        return value + 2**bit * (1 - 2 * ((value // 2**bit) % 2))

    barrier = pltpu.get_barrier_semaphore()

    def greet(to_p, to_q):
        pl.semaphore_signal(
            barrier, inc=1, device_id=(to_p, to_q), device_id_type=pl.DeviceIdType.MESH
        )

    greet(pair, q)
    for bit in range(bits):
        greet(p, flipped(q, bit))

    @pl.when(has_next)
    def _():
        greet(p + 2, q)

    @pl.when(p >= 2)
    def _():
        greet(p - 2, q)

    chain = jnp.where(has_next, 1, 0) + jnp.where(p >= 2, 1, 0)
    pl.semaphore_wait(barrier, 1 + bits + chain)

    def remote(ref, send, recv, to_p, to_q):
        return pltpu.make_async_remote_copy(
            src_ref=ref,
            dst_ref=ref,
            send_sem=send,
            recv_sem=recv,
            device_id=(to_p, to_q),
            device_id_type=pl.DeviceIdType.MESH,
        )

    def c_local(b):
        return pltpu.make_async_copy(across.at[b], c_out.at[own, b], c_recv.at[own, b])

    def c_next(b):
        return remote(c_out.at[own, b], z_send.at[b], c_recv.at[own, b], p + 2, q)

    def c_pair(b):
        return remote(c_out.at[own, b], pair_send.at[b], c_recv.at[own, b], pair, q)

    def c_arrived(k, b):
        pltpu.make_async_copy(across.at[b], c_out.at[k, b], c_recv.at[k, b]).wait()

    order = [q, flipped(q, 0)]

    def r_local(k, a):
        source = column.at[a] if a < lbr else c_out.at[a - lbr, 0]
        return pltpu.make_async_copy(source, r_out.at[k, a], r_recv.at[k, a])

    def r_child(k, a, bit):
        to_q = flipped(q, bit)
        return remote(r_out.at[k, a], r_send.at[k, a, bit], r_recv.at[k, a], p, to_q)

    def sends(k, bit):
        return order[k] % 2 ** (bit + 1) == 0

    for k in range(STEPS):

        @pl.when(order[k] == 0)
        def _():
            for a in range(lbr):
                r_local(k, a).start()

    @pl.when(p < 2)
    def _():
        for b in range(lbc):
            c_local(b).start()

    for s in range(max(lbc, lbr + STEPS)):
        if s < lbc:
            c_arrived(own, s)

            @pl.when(has_next)
            def _():
                c_next(s).start()

            c_pair(s).start()
        if s == lbr:
            c_arrived(other, 0)
            for k in range(STEPS):

                @pl.when(order[k] == 0)
                def _():
                    for a in range(lbr, lbr + STEPS):
                        r_local(k, a).start()

        if s < lbr + STEPS:
            for k in range(STEPS):
                r_local(k, s).wait()
                for bit in reversed(range(bits)):

                    @pl.when(sends(k, bit))
                    def _():
                        r_child(k, s, bit).start()

    for b in range(1, lbc):
        c_arrived(other, b)
    for b in range(lbc):
        c_pair(b).wait_send()

        @pl.when(has_next)
        def _():
            c_next(b).wait_send()

    for k in range(STEPS):
        for bit in range(bits):

            @pl.when(sends(k, bit))
            def _():
                for a in range(lbr + STEPS):
                    r_child(k, a, bit).wait_send()


def exchange(column, across, rows, cols):
    lbr, blk, _ = column.shape
    lbc = across.shape[0]
    bits = cols.bit_length() - 1
    anywhere = pl.BlockSpec(memory_space=pl.ANY)
    return pl.pallas_call(
        functools.partial(copy_kernel, rows, cols),
        out_shape=(
            jax.ShapeDtypeStruct((STEPS, lbr + STEPS, blk, blk), jnp.float32),
            jax.ShapeDtypeStruct((STEPS, lbc, blk, blk), jnp.float32),
        ),
        in_specs=[anywhere, anywhere],
        out_specs=(anywhere, anywhere),
        scratch_shapes=[
            pltpu.SemaphoreType.DMA((STEPS, lbr + STEPS)),
            pltpu.SemaphoreType.DMA((STEPS, lbc)),
            pltpu.SemaphoreType.DMA((STEPS, lbr + STEPS, bits)),
            pltpu.SemaphoreType.DMA((lbc,)),
            pltpu.SemaphoreType.DMA((lbc,)),
        ],
        compiler_params=pltpu.CompilerParams(collective_id=0, has_side_effects=True),
    )(column, across)


def on_device(kernel):
    rows = lax.axis_size("prow")
    lbr, blk, lbc = (kernel.shape[0], kernel.shape[2], kernel.shape[3])
    flat = kernel.reshape(lbr * blk * lbc * (blk // TILE), TILE)
    column = kernel[:, 0, :, 0, 0, :]
    across = kernel[0, 0, :, :, 0, :].transpose(1, 0, 2)

    row_panel, col_panel = exchange(column, across, rows, lax.axis_size("pcol"))
    d00, d10 = row_panel[0, lbr], row_panel[0, lbr + 1]
    diag = jnp.block([[d00, jnp.zeros_like(d00)], [d10, row_panel[1, lbr + 1]]])
    lower, inverse = factor(diag)
    out = update(flat, row_panel, col_panel, inverse, lower, rows)
    return out.reshape(kernel.shape)


def solution(mesh):
    in_specs = (P(None, "prow", None, None, "pcol", None),)
    out_specs = P(None, "prow", None, None, "pcol", None)
    return jax.shard_map(
        on_device, mesh=mesh, in_specs=in_specs, out_specs=out_specs, check_vma=False
    )
```

```python
import functools

import jax
import jax.numpy as jnp
from jax import lax
from jax.experimental import pallas as pl
from jax.experimental.pallas import tpu as pltpu
from jax.sharding import PartitionSpec as P

STEPS = 2
TILE = 128
SUB = 8
HIGH = lax.Precision.HIGHEST


def dot_nn(a, b):
    return lax.dot_general(
        a, b, (((1,), (0,)), ((), ())), precision=HIGH, preferred_element_type=jnp.float32
    )


def dot_nt(a, b):
    return lax.dot_general(
        a, b, (((1,), (1,)), ((), ())), precision=HIGH, preferred_element_type=jnp.float32
    )


def split(x):
    hi = x.astype(jnp.bfloat16)
    lo = (x - hi.astype(jnp.float32)).astype(jnp.bfloat16)
    return hi, lo


def factor_tile(tile):
    count = TILE // SUB
    row = lax.broadcasted_iota(jnp.int32, (SUB, TILE), 0)
    lane = lax.broadcasted_iota(jnp.int32, (SUB, TILE), 1)
    upper = [tile[SUB * r : SUB * (r + 1), :] for r in range(count)]
    inverse = [jnp.where(lane == row + SUB * r, 1.0, 0.0) for r in range(count)]
    for g in range(count):
        cols = [
            [
                jnp.broadcast_to(upper[r][:, SUB * g + j : SUB * g + j + 1], (SUB, TILE))
                for r in range(g, count)
            ]
            for j in range(SUB)
        ]
        scale = jnp.zeros((SUB, TILE), jnp.float32)
        for j in range(SUB):
            pivot = jnp.broadcast_to(cols[j][0][j : j + 1, :], (SUB, TILE))
            scale = jnp.where(row == j, pivot, scale)
            recip = 1.0 / pivot
            row_u = jnp.broadcast_to(upper[g][j : j + 1, :], (SUB, TILE)) * recip
            row_i = jnp.broadcast_to(inverse[g][j : j + 1, :], (SUB, TILE)) * recip
            heads = [
                jnp.broadcast_to(cols[j2][0][j : j + 1, :], (SUB, TILE)) * recip
                for j2 in range(j + 1, SUB)
            ]
            for r in range(g, count):
                f = cols[j][r - g]
                if r == g:
                    f = jnp.where(row > j, f, 0.0)
                upper[r] = upper[r] - f * row_u
                inverse[r] = inverse[r] - f * row_i
                for j2 in range(j + 1, SUB):
                    cols[j2][r - g] = cols[j2][r - g] - f * heads[j2 - j - 1]
        root = lax.rsqrt(scale)
        upper[g] = jnp.where(lane >= row + SUB * g, upper[g] * root, 0.0)
        inverse[g] = jnp.where(lane <= row + SUB * g, inverse[g] * root, 0.0)
    return jnp.concatenate(upper, axis=0), jnp.concatenate(inverse, axis=0)


def factor_kernel(d_ref, l_ref, w_ref, work):
    n = d_ref.shape[0]
    work[...] = d_ref[...]
    l_ref[...] = jnp.zeros_like(l_ref)
    w_ref[...] = jnp.where(
        lax.broadcasted_iota(jnp.int32, (n, n), 0) == lax.broadcasted_iota(jnp.int32, (n, n), 1),
        1.0,
        0.0,
    )
    rows = lax.broadcasted_iota(jnp.int32, (n, TILE), 0)

    def step(t, carry):
        at = pl.ds(pl.multiple_of(t * TILE, TILE), TILE)
        upper, inverse = factor_tile(work[at, at])
        panel = dot_nt(work[:, at], inverse)
        below = jnp.where(rows >= (t + 1) * TILE, panel, 0.0)
        l_ref[:, at] = below
        l_ref[at, at] = upper.T
        work[...] = work[...] - dot_nt(below, below)
        head = dot_nn(inverse, w_ref[at, :])
        w_ref[...] = w_ref[...] - dot_nn(below, head)
        w_ref[at, :] = head
        return carry

    lax.fori_loop(0, n // TILE, step, 0)


def factor(diag):
    n = diag.shape[0]
    out = jax.ShapeDtypeStruct((n, n), jnp.float32)
    return pl.pallas_call(
        factor_kernel,
        out_shape=(out, out),
        in_specs=[pl.BlockSpec(memory_space=pltpu.VMEM)],
        out_specs=(pl.BlockSpec(memory_space=pltpu.VMEM),) * 2,
        scratch_shapes=[pltpu.VMEM((n, n), jnp.float32)],
        compiler_params=pltpu.CompilerParams(vmem_limit_bytes=32 * 2**20),
        cost_estimate=pl.CostEstimate(flops=2 * n**3, bytes_accessed=12 * n * n, transcendentals=0),
    )(diag)


def update_kernel(rows, blk, lbc, m_ref, r_ref, c_ref, w_ref, l_ref, out_ref, cols):
    a = pl.program_id(0)
    row_id = a * rows + lax.axis_index("prow")
    q = lax.axis_index("pcol")
    lanes = blk // TILE
    pitch = lbc * lanes
    depth = STEPS * blk

    @pl.when(a == 0)
    def _():
        def prepare(b, carry):
            raw = jnp.concatenate([c_ref[k, b] for k in range(STEPS)], axis=0)
            for k in range(STEPS):
                at, used = k * blk, (k + 1) * blk
                hi, lo = split(dot_nn(w_ref[at:used, :used], raw[:used]))
                cols[b, at:used, :] = hi
                cols[b, depth + at : depth + used, :] = hi
                cols[b, 2 * depth + at : 2 * depth + used, :] = lo
            return carry

        lax.fori_loop(0, lbc, prepare, 0)

    def store(b, value):
        for h in range(lanes):
            at = pl.ds(lanes * b + h, blk, stride=pitch)
            out_ref[at, :] = value[:, h * TILE : (h + 1) * TILE]

    @pl.when(row_id < STEPS)
    def _():
        out_ref[...] = jnp.zeros_like(out_ref)
        for i in range(STEPS):
            for j in range(i + 1):

                @pl.when((row_id == i) & (q == j))
                def _():
                    store(0, l_ref[i * blk : (i + 1) * blk, j * blk : (j + 1) * blk])

    @pl.when(row_id >= STEPS)
    def _():
        raw = jnp.concatenate([r_ref[k, 0] for k in range(STEPS)], axis=1)
        parts = []
        for k in range(STEPS):
            at, used = k * blk, (k + 1) * blk
            parts.append(dot_nt(raw[:, :used], w_ref[at:used, :used]))
        panel = jnp.concatenate(parts, axis=1)
        hi, lo = split(panel)
        left = jnp.concatenate([hi, lo, hi], axis=1)
        for b in range(lbc):
            delta = jnp.dot(left, cols[b], preferred_element_type=jnp.float32)
            for h in range(lanes):
                at = pl.ds(lanes * b + h, blk, stride=pitch)
                out_ref[at, :] = m_ref[at, :] - delta[:, h * TILE : (h + 1) * TILE]
        for j in range(STEPS):

            @pl.when(q == j)
            def _():
                store(0, panel[:, j * blk : (j + 1) * blk])


def update(flat, row_panel, col_panel, inverse, lower, rows):
    blk = row_panel.shape[2]
    lbc = col_panel.shape[1]
    depth = STEPS * blk
    stripe = blk * lbc * (blk // TILE)
    lbr = flat.shape[0] // stripe
    whole = pl.BlockSpec((depth, depth), lambda a: (0, 0))
    return pl.pallas_call(
        functools.partial(update_kernel, rows, blk, lbc),
        grid=(lbr,),
        out_shape=jax.ShapeDtypeStruct(flat.shape, jnp.float32),
        in_specs=[
            pl.BlockSpec((stripe, TILE), lambda a: (a, 0)),
            pl.BlockSpec((STEPS, 1, blk, blk), lambda a: (0, a, 0, 0)),
            pl.BlockSpec((STEPS, lbc, blk, blk), lambda a: (0, 0, 0, 0)),
            whole,
            whole,
        ],
        out_specs=pl.BlockSpec((stripe, TILE), lambda a: (a, 0)),
        scratch_shapes=[pltpu.VMEM((lbc, 3 * depth, blk), jnp.bfloat16)],
        compiler_params=pltpu.CompilerParams(vmem_limit_bytes=56 * 2**20),
        cost_estimate=pl.CostEstimate(
            flops=6 * flat.size * depth, bytes_accessed=8 * flat.size, transcendentals=0
        ),
    )(flat, row_panel, col_panel, inverse, lower)


def copy_kernel(rows, cols, column, across, r_out, c_out, r_recv, c_recv, r_send, z_send, pair_send):
    lbr, lbc = column.shape[0], across.shape[0]
    bits = cols.bit_length() - 1
    p = lax.axis_index("prow")
    q = lax.axis_index("pcol")
    own = p % 2
    other = 1 - own
    pair = p + 1 - 2 * own
    has_next = p + 2 < rows

    def flipped(value, bit):
        return value + 2**bit * (1 - 2 * ((value // 2**bit) % 2))

    barrier = pltpu.get_barrier_semaphore()

    def greet(to_p, to_q):
        pl.semaphore_signal(
            barrier, inc=1, device_id=(to_p, to_q), device_id_type=pl.DeviceIdType.MESH
        )

    greet(pair, q)
    for bit in range(bits):
        greet(p, flipped(q, bit))

    @pl.when(has_next)
    def _():
        greet(p + 2, q)

    @pl.when(p >= 2)
    def _():
        greet(p - 2, q)

    chain = jnp.where(has_next, 1, 0) + jnp.where(p >= 2, 1, 0)
    pl.semaphore_wait(barrier, 1 + bits + chain)

    def remote(ref, send, recv, to_p, to_q):
        return pltpu.make_async_remote_copy(
            src_ref=ref,
            dst_ref=ref,
            send_sem=send,
            recv_sem=recv,
            device_id=(to_p, to_q),
            device_id_type=pl.DeviceIdType.MESH,
        )

    def c_local(b):
        return pltpu.make_async_copy(across.at[b], c_out.at[own, b], c_recv.at[own, b])

    def c_next(b):
        return remote(c_out.at[own, b], z_send.at[b], c_recv.at[own, b], p + 2, q)

    def c_pair(b):
        return remote(c_out.at[own, b], pair_send.at[b], c_recv.at[own, b], pair, q)

    def c_arrived(k, b):
        pltpu.make_async_copy(across.at[b], c_out.at[k, b], c_recv.at[k, b]).wait()

    order = [q, flipped(q, 0)]

    def r_local(k, a):
        source = column.at[a] if a < lbr else c_out.at[a - lbr, 0]
        return pltpu.make_async_copy(source, r_out.at[k, a], r_recv.at[k, a])

    def r_child(k, a, bit):
        to_q = flipped(q, bit)
        return remote(r_out.at[k, a], r_send.at[k, a, bit], r_recv.at[k, a], p, to_q)

    def sends(k, bit):
        return order[k] % 2 ** (bit + 1) == 0

    for k in range(STEPS):

        @pl.when(order[k] == 0)
        def _():
            for a in range(lbr):
                r_local(k, a).start()

    @pl.when(p < 2)
    def _():
        for b in range(lbc):
            c_local(b).start()

    for s in range(max(lbc, lbr + STEPS)):
        if s < lbc:
            c_arrived(own, s)

            @pl.when(has_next)
            def _():
                c_next(s).start()

            c_pair(s).start()
        if s == lbr:
            c_arrived(other, 0)
            for k in range(STEPS):

                @pl.when(order[k] == 0)
                def _():
                    for a in range(lbr, lbr + STEPS):
                        r_local(k, a).start()

        if s < lbr + STEPS:
            for k in range(STEPS):

                @pl.when(order[k] % 2 == 0)
                def _():
                    r_local(k, s).wait()

                for bit in reversed(range(bits)):

                    @pl.when(sends(k, bit))
                    def _():
                        r_child(k, s, bit).start()

    for k in range(STEPS):

        @pl.when(order[k] % 2 == 1)
        def _():
            for a in range(lbr + STEPS):
                r_local(k, a).wait()

    for b in range(1, lbc):
        c_arrived(other, b)
    for b in range(lbc):
        c_pair(b).wait_send()

        @pl.when(has_next)
        def _():
            c_next(b).wait_send()

    for k in range(STEPS):
        for bit in range(bits):

            @pl.when(sends(k, bit))
            def _():
                for a in range(lbr + STEPS):
                    r_child(k, a, bit).wait_send()


def exchange(column, across, rows, cols):
    lbr, blk, _ = column.shape
    lbc = across.shape[0]
    bits = cols.bit_length() - 1
    anywhere = pl.BlockSpec(memory_space=pl.ANY)
    return pl.pallas_call(
        functools.partial(copy_kernel, rows, cols),
        out_shape=(
            jax.ShapeDtypeStruct((STEPS, lbr + STEPS, blk, blk), jnp.float32),
            jax.ShapeDtypeStruct((STEPS, lbc, blk, blk), jnp.float32),
        ),
        in_specs=[anywhere, anywhere],
        out_specs=(anywhere, anywhere),
        scratch_shapes=[
            pltpu.SemaphoreType.DMA((STEPS, lbr + STEPS)),
            pltpu.SemaphoreType.DMA((STEPS, lbc)),
            pltpu.SemaphoreType.DMA((STEPS, lbr + STEPS, bits)),
            pltpu.SemaphoreType.DMA((lbc,)),
            pltpu.SemaphoreType.DMA((lbc,)),
        ],
        compiler_params=pltpu.CompilerParams(collective_id=0, has_side_effects=True),
    )(column, across)


def on_device(kernel):
    rows = lax.axis_size("prow")
    lbr, blk, lbc = (kernel.shape[0], kernel.shape[2], kernel.shape[3])
    flat = kernel.reshape(lbr * blk * lbc * (blk // TILE), TILE)
    column = kernel[:, 0, :, 0, 0, :]
    across = kernel[0, 0, :, :, 0, :].transpose(1, 0, 2)

    row_panel, col_panel = exchange(column, across, rows, lax.axis_size("pcol"))
    d00, d10 = row_panel[0, lbr], row_panel[0, lbr + 1]
    diag = jnp.block([[d00, jnp.zeros_like(d00)], [d10, row_panel[1, lbr + 1]]])
    lower, inverse = factor(diag)
    out = update(flat, row_panel, col_panel, inverse, lower, rows)
    return out.reshape(kernel.shape)


def solution(mesh):
    in_specs = (P(None, "prow", None, None, "pcol", None),)
    out_specs = P(None, "prow", None, None, "pcol", None)
    return jax.shard_map(
        on_device, mesh=mesh, in_specs=in_specs, out_specs=out_specs, check_vma=False
    )
```

```python
import functools

import jax
import jax.numpy as jnp
from jax import lax
from jax.experimental import pallas as pl
from jax.experimental.pallas import tpu as pltpu
from jax.sharding import PartitionSpec as P

STEPS = 2
TILE = 128
SUB = 8
HIGH = lax.Precision.HIGHEST


def dot_nn(a, b):
    return lax.dot_general(
        a, b, (((1,), (0,)), ((), ())), precision=HIGH, preferred_element_type=jnp.float32
    )


def dot_nt(a, b):
    return lax.dot_general(
        a, b, (((1,), (1,)), ((), ())), precision=HIGH, preferred_element_type=jnp.float32
    )


def split(x):
    hi = x.astype(jnp.bfloat16)
    lo = (x - hi.astype(jnp.float32)).astype(jnp.bfloat16)
    return hi, lo


def factor_tile(tile):
    count = TILE // SUB
    row = lax.broadcasted_iota(jnp.int32, (SUB, TILE), 0)
    lane = lax.broadcasted_iota(jnp.int32, (SUB, TILE), 1)
    upper = [tile[SUB * r : SUB * (r + 1), :] for r in range(count)]
    inverse = [jnp.where(lane == row + SUB * r, 1.0, 0.0) for r in range(count)]
    for g in range(count):
        cols = [
            [
                jnp.broadcast_to(upper[r][:, SUB * g + j : SUB * g + j + 1], (SUB, TILE))
                for r in range(g, count)
            ]
            for j in range(SUB)
        ]
        scale = jnp.zeros((SUB, TILE), jnp.float32)
        for j in range(SUB):
            pivot = jnp.broadcast_to(cols[j][0][j : j + 1, :], (SUB, TILE))
            scale = jnp.where(row == j, pivot, scale)
            recip = 1.0 / pivot
            row_u = jnp.broadcast_to(upper[g][j : j + 1, :], (SUB, TILE)) * recip
            row_i = jnp.broadcast_to(inverse[g][j : j + 1, :], (SUB, TILE)) * recip
            heads = [
                jnp.broadcast_to(cols[j2][0][j : j + 1, :], (SUB, TILE)) * recip
                for j2 in range(j + 1, SUB)
            ]
            for r in range(g, count):
                f = cols[j][r - g]
                if r == g:
                    f = jnp.where(row > j, f, 0.0)
                upper[r] = upper[r] - f * row_u
                inverse[r] = inverse[r] - f * row_i
                for j2 in range(j + 1, SUB):
                    cols[j2][r - g] = cols[j2][r - g] - f * heads[j2 - j - 1]
        root = lax.rsqrt(scale)
        upper[g] = jnp.where(lane >= row + SUB * g, upper[g] * root, 0.0)
        inverse[g] = jnp.where(lane <= row + SUB * g, inverse[g] * root, 0.0)
    return jnp.concatenate(upper, axis=0), jnp.concatenate(inverse, axis=0)


def factor_kernel(d_ref, l_ref, w_ref, work):
    n = d_ref.shape[0]
    work[...] = d_ref[...]
    l_ref[...] = jnp.zeros_like(l_ref)
    w_ref[...] = jnp.where(
        lax.broadcasted_iota(jnp.int32, (n, n), 0) == lax.broadcasted_iota(jnp.int32, (n, n), 1),
        1.0,
        0.0,
    )
    rows = lax.broadcasted_iota(jnp.int32, (n, TILE), 0)

    def step(t, carry):
        at = pl.ds(pl.multiple_of(t * TILE, TILE), TILE)
        upper, inverse = factor_tile(work[at, at])
        panel = dot_nt(work[:, at], inverse)
        below = jnp.where(rows >= (t + 1) * TILE, panel, 0.0)
        l_ref[:, at] = below
        l_ref[at, at] = upper.T
        work[...] = work[...] - dot_nt(below, below)
        head = dot_nn(inverse, w_ref[at, :])
        w_ref[...] = w_ref[...] - dot_nn(below, head)
        w_ref[at, :] = head
        return carry

    lax.fori_loop(0, n // TILE, step, 0)


def factor(diag):
    n = diag.shape[0]
    out = jax.ShapeDtypeStruct((n, n), jnp.float32)
    return pl.pallas_call(
        factor_kernel,
        out_shape=(out, out),
        in_specs=[pl.BlockSpec(memory_space=pltpu.VMEM)],
        out_specs=(pl.BlockSpec(memory_space=pltpu.VMEM),) * 2,
        scratch_shapes=[pltpu.VMEM((n, n), jnp.float32)],
        compiler_params=pltpu.CompilerParams(vmem_limit_bytes=32 * 2**20),
        cost_estimate=pl.CostEstimate(flops=2 * n**3, bytes_accessed=12 * n * n, transcendentals=0),
    )(diag)


def update_kernel(rows, blk, lbc, m_ref, r_ref, c_ref, w_ref, l_ref, out_ref, cols):
    a = pl.program_id(0)
    row_id = a * rows + lax.axis_index("prow")
    q = lax.axis_index("pcol")
    lanes = blk // TILE
    pitch = lbc * lanes
    depth = STEPS * blk

    @pl.when(a == 0)
    def _():
        def prepare(b, carry):
            raw = jnp.concatenate([c_ref[k, b] for k in range(STEPS)], axis=0)
            for k in range(STEPS):
                at, used = k * blk, (k + 1) * blk
                hi, lo = split(dot_nn(w_ref[at:used, :used], raw[:used]))
                cols[b, at:used, :] = hi
                cols[b, depth + at : depth + used, :] = hi
                cols[b, 2 * depth + at : 2 * depth + used, :] = lo
            return carry

        lax.fori_loop(0, lbc, prepare, 0)

    def store(b, value):
        for h in range(lanes):
            at = pl.ds(lanes * b + h, blk, stride=pitch)
            out_ref[at, :] = value[:, h * TILE : (h + 1) * TILE]

    @pl.when(row_id < STEPS)
    def _():
        out_ref[...] = jnp.zeros_like(out_ref)
        for i in range(STEPS):
            for j in range(i + 1):

                @pl.when((row_id == i) & (q == j))
                def _():
                    store(0, l_ref[i * blk : (i + 1) * blk, j * blk : (j + 1) * blk])

    @pl.when(row_id >= STEPS)
    def _():
        raw = jnp.concatenate([r_ref[k, 0] for k in range(STEPS)], axis=1)
        parts = []
        for k in range(STEPS):
            at, used = k * blk, (k + 1) * blk
            parts.append(dot_nt(raw[:, :used], w_ref[at:used, :used]))
        panel = jnp.concatenate(parts, axis=1)
        hi, lo = split(panel)
        left = jnp.concatenate([hi, lo, hi], axis=1)
        for b in range(lbc):
            delta = jnp.dot(left, cols[b], preferred_element_type=jnp.float32)
            for h in range(lanes):
                at = pl.ds(lanes * b + h, blk, stride=pitch)
                out_ref[at, :] = m_ref[at, :] - delta[:, h * TILE : (h + 1) * TILE]
        for j in range(STEPS):

            @pl.when(q == j)
            def _():
                store(0, panel[:, j * blk : (j + 1) * blk])


def update(flat, row_panel, col_panel, inverse, lower, rows):
    blk = row_panel.shape[2]
    lbc = col_panel.shape[1]
    depth = STEPS * blk
    stripe = blk * lbc * (blk // TILE)
    lbr = flat.shape[0] // stripe
    whole = pl.BlockSpec((depth, depth), lambda a: (0, 0))
    return pl.pallas_call(
        functools.partial(update_kernel, rows, blk, lbc),
        grid=(lbr,),
        out_shape=jax.ShapeDtypeStruct(flat.shape, jnp.float32),
        in_specs=[
            pl.BlockSpec((stripe, TILE), lambda a: (a, 0)),
            pl.BlockSpec((STEPS, 1, blk, blk), lambda a: (0, a, 0, 0)),
            pl.BlockSpec((STEPS, lbc, blk, blk), lambda a: (0, 0, 0, 0)),
            whole,
            whole,
        ],
        out_specs=pl.BlockSpec((stripe, TILE), lambda a: (a, 0)),
        scratch_shapes=[pltpu.VMEM((lbc, 3 * depth, blk), jnp.bfloat16)],
        compiler_params=pltpu.CompilerParams(vmem_limit_bytes=56 * 2**20),
        cost_estimate=pl.CostEstimate(
            flops=6 * flat.size * depth, bytes_accessed=8 * flat.size, transcendentals=0
        ),
    )(flat, row_panel, col_panel, inverse, lower)


def copy_kernel(rows, cols, column, across, r_out, c_out, r_recv, c_recv, r_send, z_send, pair_send):
    lbr, lbc = column.shape[0], across.shape[0]
    bits = cols.bit_length() - 1
    p = lax.axis_index("prow")
    q = lax.axis_index("pcol")
    own = p % 2
    other = 1 - own
    pair = p + 1 - 2 * own
    has_next = p + 2 < rows

    def flipped(value, bit):
        return value + 2**bit * (1 - 2 * ((value // 2**bit) % 2))

    barrier = pltpu.get_barrier_semaphore()

    def greet(to_p, to_q):
        pl.semaphore_signal(
            barrier, inc=1, device_id=(to_p, to_q), device_id_type=pl.DeviceIdType.MESH
        )

    greet(pair, q)
    for bit in range(bits):
        greet(p, flipped(q, bit))

    @pl.when(has_next)
    def _():
        greet(p + 2, q)

    @pl.when(p >= 2)
    def _():
        greet(p - 2, q)

    chain = jnp.where(has_next, 1, 0) + jnp.where(p >= 2, 1, 0)
    pl.semaphore_wait(barrier, 1 + bits + chain)

    def remote(ref, send, recv, to_p, to_q):
        return pltpu.make_async_remote_copy(
            src_ref=ref,
            dst_ref=ref,
            send_sem=send,
            recv_sem=recv,
            device_id=(to_p, to_q),
            device_id_type=pl.DeviceIdType.MESH,
        )

    def c_local(b):
        return pltpu.make_async_copy(across.at[b], c_out.at[own, b], c_recv.at[own, b])

    def c_next(b):
        return remote(c_out.at[own, b], z_send.at[b], c_recv.at[own, b], p + 2, q)

    def c_pair(b):
        return remote(c_out.at[own, b], pair_send.at[b], c_recv.at[own, b], pair, q)

    def c_arrived(k, b):
        pltpu.make_async_copy(across.at[b], c_out.at[k, b], c_recv.at[k, b]).wait()

    order = [q, flipped(q, 0)]

    def r_local(k, a):
        source = column.at[a] if a < lbr else c_out.at[a - lbr, 0]
        return pltpu.make_async_copy(source, r_out.at[k, a], r_recv.at[k, a])

    def r_child(k, a, bit):
        to_q = flipped(q, bit)
        return remote(r_out.at[k, a], r_send.at[k, a, bit], r_recv.at[k, a], p, to_q)

    def sends(k, bit):
        return order[k] % 2 ** (bit + 1) == 0

    for k in range(STEPS):

        @pl.when(order[k] == 0)
        def _():
            for a in range(lbr):
                r_local(k, a).start()

    @pl.when(p < 2)
    def _():
        for b in range(lbc):
            c_local(b).start()

    for s in range(max(lbc, lbr + STEPS)):
        if s < lbc:
            c_arrived(own, s)

            @pl.when(has_next)
            def _():
                c_next(s).start()

            c_pair(s).start()
        if s == lbr:
            c_arrived(other, 0)
            for k in range(STEPS):

                @pl.when(order[k] == 0)
                def _():
                    for a in range(lbr, lbr + STEPS):
                        r_local(k, a).start()

        if s < lbr + STEPS:
            for k in range(STEPS):

                @pl.when(order[k] % 2 == 0)
                def _():
                    r_local(k, s).wait()

                for bit in reversed(range(bits)):

                    @pl.when(sends(k, bit))
                    def _():
                        r_child(k, s, bit).start()

    for k in range(STEPS):

        @pl.when(order[k] % 2 == 1)
        def _():
            for a in range(lbr + STEPS):
                r_local(k, a).wait()

    for b in range(1, lbc):
        c_arrived(other, b)
    for b in range(lbc):
        c_pair(b).wait_send()

        @pl.when(has_next)
        def _():
            c_next(b).wait_send()

    for k in range(STEPS):
        for bit in range(bits):

            @pl.when(sends(k, bit))
            def _():
                for a in range(lbr + STEPS):
                    r_child(k, a, bit).wait_send()


def exchange(column, across, rows, cols):
    lbr, blk, _ = column.shape
    lbc = across.shape[0]
    bits = cols.bit_length() - 1
    held = pl.BlockSpec(memory_space=pltpu.VMEM)
    return pl.pallas_call(
        functools.partial(copy_kernel, rows, cols),
        out_shape=(
            jax.ShapeDtypeStruct((STEPS, lbr + STEPS, blk, blk), jnp.float32),
            jax.ShapeDtypeStruct((STEPS, lbc, blk, blk), jnp.float32),
        ),
        in_specs=[held, held],
        out_specs=(held, held),
        scratch_shapes=[
            pltpu.SemaphoreType.DMA((STEPS, lbr + STEPS)),
            pltpu.SemaphoreType.DMA((STEPS, lbc)),
            pltpu.SemaphoreType.DMA((STEPS, lbr + STEPS, bits)),
            pltpu.SemaphoreType.DMA((lbc,)),
            pltpu.SemaphoreType.DMA((lbc,)),
        ],
        compiler_params=pltpu.CompilerParams(
            collective_id=0, has_side_effects=True, vmem_limit_bytes=40 * 2**20
        ),
    )(column, across)


def on_device(kernel):
    rows = lax.axis_size("prow")
    lbr, blk, lbc = (kernel.shape[0], kernel.shape[2], kernel.shape[3])
    flat = kernel.reshape(lbr * blk * lbc * (blk // TILE), TILE)
    column = kernel[:, 0, :, 0, 0, :]
    across = kernel[0, 0, :, :, 0, :].transpose(1, 0, 2)

    row_panel, col_panel = exchange(column, across, rows, lax.axis_size("pcol"))
    d00, d10 = row_panel[0, lbr], row_panel[0, lbr + 1]
    diag = jnp.block([[d00, jnp.zeros_like(d00)], [d10, row_panel[1, lbr + 1]]])
    lower, inverse = factor(diag)
    out = update(flat, row_panel, col_panel, inverse, lower, rows)
    return out.reshape(kernel.shape)


def solution(mesh):
    in_specs = (P(None, "prow", None, None, "pcol", None),)
    out_specs = P(None, "prow", None, None, "pcol", None)
    return jax.shard_map(
        on_device, mesh=mesh, in_specs=in_specs, out_specs=out_specs, check_vma=False
    )
```
